32 devices in a mesh: freq: 4 (over x, core), mode: 8 (over z, y).
Axes of the slice: x: 2, y: 2, z: 4, core: 2. Of those that a mesh axis runs over, the one named last changes fastest.
Arguments:
- mode_shapes: bfloat16 [6144, 3072], P(None, 'mode'), may hold values from -0.15625 to 0.15625
- modal_freq: float32 [3072], P('mode'), may hold values from 0.5 to 4
- damping: float32 [3072], P('mode'), may hold values from 0.05 to 0.2
- excitation: float32 [16], P('freq'), parts along dimension 0, may hold values from 0.5 to 4
- modal_load: float32 [3072, 16, 2, 64], P('mode', 'freq'), parts along dimension 1, may hold values from -6 to 6
- attach: int32 [8, 96], replicated, may hold values from 0 to 6143
- row_count: int32 [8], P('mode'), may hold values from 48 to 384, as said below
- otm: bfloat16 [8, 384, 96], P('mode'), may hold values from -0.625 to 0.625
Outputs:
- csd: bfloat16 [8, 16, 2, 384, 384], P('mode', 'freq'), parts along dimension 1
- joint_csd: bfloat16 [8, 16, 2, 128, 384], P('mode', 'freq'), parts along dimension 1
The draws below stay inside these ranges and needn't reach their ends.
There are 4 independent parts, one for each index of `freq`. The reference program is written for one: setup_inputs(seed, part) draws one part's arguments, and reference() takes and returns one part's arrays. A program takes and returns all parts, laid end to end along the dimension named above; an argument that names none is the same for every part. Nothing has to cross between parts.
Inputs may be any that keep to these rules, and one draw needn't show every extreme that they name: `row_count`: at least one component has exactly 384 rows in every draw.
All inputs are finite; a program needn't handle non-finite values.
Results may differ from the reference program's by a relative error of at most 0.008.
Values may be sent and summed in bfloat16 or wider, within the bound.
No kernel may reach another device: no remote copies, remote signals or barrier semaphores. Data moves between devices by JAX's collectives and lax.ppermute only.
A program may use at most 128 MiB of HBM per device.

```python
import math
import jax
import jax.numpy as jnp

MODES = 3072
IFACE = 6144
K = 64
FREQ_PART = 4
COMPS = 8
ATT = 96
ROWS_MAX = 384
CROSS = 128


def draw_row_count(key, part):
    base_key = jax.random.fold_in(key, 11)
    first_key, second_key = jax.random.split(base_key)
    spread = jax.random.randint(first_key, (COMPS,), 0, 64)
    lowest = ROWS_MAX // 8
    counts = lowest + spread * spread * (ROWS_MAX - lowest) // 3969
    chosen = jax.random.randint(second_key, (), 0, COMPS)
    counts = jnp.where(jnp.arange(COMPS) == chosen, ROWS_MAX, counts)
    return counts.astype(jnp.int32)


def plant(drawn, stream_key, least, top_value):
    dims = drawn.shape
    spot = [jax.random.randint(jax.random.fold_in(stream_key, axis), (), 0, dims[axis]) for axis in range(len(dims))]
    drawn = drawn.at[tuple(spot)].set(least)
    longest = dims.index(max(dims))
    spot[longest] = (spot[longest] + 1) % dims[longest]
    return drawn.at[tuple(spot)].set(top_value)


def strengthened(entries, rng, source, target, blocks, factor):
    owner, partner = [(jnp.arange(entries.shape[position]) // (entries.shape[position] // blocks)).reshape([-1 if axis == position else 1 for axis in range(entries.ndim)]) for position in (source, target)]
    chosen = jax.random.permutation(rng, blocks)[partner]
    strong = (owner == chosen) | (owner == (partner + blocks // 2) % blocks)
    return jnp.where(strong, factor * entries, entries)


def shard_levels(own_key, shape, cuts, least, top_value):
    def one(position, shards_of):
        draws = jax.random.uniform(jax.random.fold_in(jax.random.fold_in(own_key, 6), position), (shards_of,), jnp.float32, least / len(cuts), top_value / len(cuts))
        return jnp.repeat(jnp.exp(draws), shape[position] // shards_of).reshape((-1,) + (1,) * (len(shape) - position - 1))

    level = one(*cuts[0])
    for cut in cuts[1:]:
        level = level * one(*cut)
    return level


def normal_values(rng, extent, width, limit, cuts=(), held_as=jnp.bfloat16):
    values = width * jax.random.normal(rng, extent, jnp.float32)
    if cuts:
        values = values * shard_levels(rng, extent, cuts, -0.22, 0.18)
    return jnp.clip(values, -limit, limit).astype(held_as)


def noise_with(rng, shape, scale, limit, cuts, heavy, held_as=jnp.bfloat16):
    result = scale * jax.random.normal(rng, shape, jnp.float32)
    if cuts:
        result = result * shard_levels(rng, shape, cuts, -0.22, 0.18)
    return jnp.clip(strengthened(result, jax.random.fold_in(rng, 3), *heavy), -limit, limit).astype(held_as)


def setup_inputs(seed: int = 0, part: int = 0) -> dict:
    key_of = jax.random.split(jax.random.key(seed), 9)
    part_keys = jax.random.split(jax.random.fold_in(key_of[8], part), 9)
    mode_shapes = noise_with(key_of[0], (IFACE, MODES), MODES ** -0.5, 0.15625, ((1, 8),), (1, 0, 8, 2.0))
    modal_freq = jnp.clip(jnp.exp(math.log(4.0) - 2.0794415 * jax.random.uniform(key_of[1], (MODES,), jnp.float32) ** shard_levels(key_of[1], (MODES,), ((0, 8),), -0.2, 0.2)), 0.5, 4.0)
    damping = jnp.clip(jnp.exp(math.log(0.2) - 1.3862944 * jax.random.uniform(key_of[2], (MODES,), jnp.float32) ** shard_levels(key_of[2], (MODES,), ((0, 8),), -0.2, 0.2)), 0.05, 0.2)
    excitation = jnp.clip(jax.random.uniform(part_keys[3], (FREQ_PART,), jnp.float32, 0.5, 4.0), 0.5, 4.0)
    modal_load = normal_values(part_keys[4], (MODES, FREQ_PART, 2, K), 1.0, 6.0, ((0, 8),), jnp.float32)
    attach = plant(jax.random.randint(key_of[5], (COMPS, ATT), 0, IFACE), jax.random.fold_in(key_of[5], 1), 0, IFACE - 1).astype(jnp.int32)
    row_count = draw_row_count(jax.random.fold_in(key_of[8], 71), part)
    otm = normal_values(key_of[7], (COMPS, ROWS_MAX, ATT), ATT ** -0.5, 0.625, ((0, 8),))
    return dict(mode_shapes=mode_shapes, modal_freq=modal_freq, damping=damping, excitation=excitation, modal_load=modal_load, attach=attach, row_count=row_count, otm=otm)


def reference(mode_shapes, modal_freq, damping, excitation, modal_load, attach, row_count, otm):
    omega_sq = modal_freq * modal_freq
    real_part = omega_sq[:, None] - (excitation * excitation)[None, :]
    imag_part = 2.0 * damping[:, None] * modal_freq[:, None] * excitation[None, :]
    denom = real_part * real_part + imag_part * imag_part
    frf_re = (omega_sq[:, None] * real_part / denom)[:, :, None]
    frf_im = (-omega_sq[:, None] * imag_part / denom)[:, :, None]
    load_re = modal_load[:, :, 0, :]
    load_im = modal_load[:, :, 1, :]
    resp_re = frf_re * load_re - frf_im * load_im
    resp_im = frf_re * load_im + frf_im * load_re
    modal_resp = jnp.stack([resp_re, resp_im], axis=2).astype(jnp.bfloat16)
    modal_resp = modal_resp.reshape(MODES, FREQ_PART * 2 * K)
    iface_resp = jnp.dot(mode_shapes, modal_resp, preferred_element_type=jnp.float32).astype(jnp.bfloat16)
    picked = jnp.take(iface_resp, attach.reshape(-1).astype(jnp.int32), axis=0).reshape(COMPS, ATT, FREQ_PART * 2 * K)
    row_mask = jnp.arange(ROWS_MAX, dtype=jnp.int32)[None, :] < row_count[:, None]
    factor = jnp.einsum("cra,caj->crj", otm.astype(jnp.float32), picked.astype(jnp.float32))
    factor = jnp.where(row_mask[:, :, None], factor, 0.0).astype(jnp.bfloat16)
    zmat = factor.reshape(COMPS, ROWS_MAX, FREQ_PART, 2 * K).astype(jnp.float32)
    wmat = jnp.concatenate([zmat[..., K:], -zmat[..., :K]], axis=-1)
    auto_re = jnp.einsum("crfk,csfk->cfrs", zmat, zmat) / K
    auto_im = jnp.einsum("crfk,csfk->cfrs", wmat, zmat) / K
    csd = jnp.stack([auto_re, auto_im], axis=2).astype(jnp.bfloat16)
    partner = jnp.concatenate([zmat[1:], jnp.zeros_like(zmat[:1])], axis=0)
    joint_re = jnp.einsum("crfk,csfk->cfrs", zmat[:, :CROSS], partner) / K
    joint_im = jnp.einsum("crfk,csfk->cfrs", wmat[:, :CROSS], partner) / K
    joint_csd = jnp.stack([joint_re, joint_im], axis=2).astype(jnp.bfloat16)
    return (csd, joint_csd)
```

```python
import functools

import jax
import jax.numpy as jnp
from jax import lax
from jax.experimental import pallas as pl
from jax.experimental.pallas import tpu as pltpu
from jax.sharding import PartitionSpec as P

CROSS = 128
CHUNKS = 12
F32 = jnp.float32
BF16 = jnp.bfloat16
NT = (((1,), (1,)), ((), ()))
TN = (((0,), (0,)), ((), ()))


def modal_response(freq_ref, damp_ref, exc_ref, load_ref, resp_ref):
    lines = load_ref.shape[0]
    width = load_ref.shape[2]
    freq = freq_ref[...]
    damp = damp_ref[...]
    omega_sq = freq * freq
    for f in range(lines):
        exc = exc_ref[f]
        a = omega_sq - exc * exc
        b = 2.0 * damp * freq * exc
        denom = a * a + b * b
        frf_re = omega_sq * a / denom
        frf_im = -omega_sq * b / denom
        load_re = load_ref[f, 0]
        load_im = load_ref[f, 1]
        base = f * 2 * width
        resp_ref[base : base + width, :] = (frf_re * load_re - frf_im * load_im).astype(BF16)
        resp_ref[base + width : base + 2 * width, :] = (
            frf_re * load_im + frf_im * load_re
        ).astype(BF16)


def fetch(shapes_ref, raw, wide, sems, start_only):
    count = sems.shape[0]
    step = raw.shape[0] // count

    def copy(i):
        rows = pl.ds(pl.multiple_of(i * step, step), step)
        return pltpu.make_async_copy(shapes_ref.at[rows, :], raw.at[rows, :], sems.at[i])

    if start_only:
        for i in range(count):
            copy(i).start()
        return

    def body(i, carry):
        copy(i).wait()
        rows = pl.ds(pl.multiple_of(i * step, step), step)
        wide[rows, :] = raw[rows, :].astype(F32)
        return carry

    lax.fori_loop(0, count, body, 0)


def product(attach_ref, wide, rows_ref, resp_ref, comp):
    count = rows_ref.shape[0]
    unroll = 16 if count % 16 == 0 else 1

    def body(b, carry):
        for u in range(unroll):
            a = b * unroll + u
            rows_ref[pl.ds(a, 1), :] = wide[pl.ds(attach_ref[comp, a], 1), :]
        return carry

    lax.fori_loop(0, count // unroll, body, 0)
    return lax.dot_general(
        rows_ref[...].astype(BF16), resp_ref[...], NT, preferred_element_type=F32
    )


def far_kernel(
    slots, attach_ref, exc_ref, freq_ref, damp_ref, load_hbm, shapes_ref, *rest
):
    outs = rest[: len(slots)]
    resp_ref, load_ref, raw, wide, rows_ref, sems, load_sem = rest[len(slots) :]
    load = pltpu.make_async_copy(load_hbm, load_ref, load_sem)
    load.start()
    fetch(shapes_ref, raw, wide, sems, True)
    me = lax.axis_index("mode")
    load.wait()
    modal_response(freq_ref, damp_ref, exc_ref, load_ref, resp_ref)
    fetch(shapes_ref, raw, wide, sems, False)
    for slot, out in zip(slots, outs):
        part = product(attach_ref, wide, rows_ref, resp_ref, jnp.bitwise_xor(me, slot))
        out[...] = part.astype(out.dtype)


def near_kernel(slots, attach_ref, resp_ref, shapes_ref, *rest):
    outs = rest[: len(slots)]
    raw, wide, rows_ref, sems = rest[len(slots) :]
    fetch(shapes_ref, raw, wide, sems, True)
    me = lax.axis_index("mode")
    fetch(shapes_ref, raw, wide, sems, False)
    for slot, out in zip(slots, outs):
        part = product(attach_ref, wide, rows_ref, resp_ref, jnp.bitwise_xor(me, slot))
        out[...] = part.astype(out.dtype)


def cross_block(left_re, left_im, right, scale):
    left = jnp.concatenate([left_re, left_im], axis=0)
    value = lax.dot_general(left, right, NT, preferred_element_type=F32) * scale
    return value.astype(BF16)


def turned(z):
    width = z.shape[1] // 2
    return jnp.concatenate([z[:, width:], -z[:, :width]], axis=1)


def auto_kernel(count_ref, otm_ref, picked_ref, csd_ref):
    rows_max = otm_ref.shape[1]
    pair = picked_ref.shape[1]
    z = lax.dot_general(otm_ref[...], picked_ref[...], TN, preferred_element_type=F32)
    keep = lax.broadcasted_iota(jnp.int32, z.shape, 0) < count_ref[0]
    z = jnp.where(keep, z, 0.0).astype(BF16)
    value = cross_block(z, turned(z), z, 2.0 / pair)
    csd_ref[0] = value[:rows_max]
    csd_ref[1] = value[rows_max:]


def joint_kernel(count_ref, otm_ref, picked_ref, next_otm_ref, next_picked_ref, joint_ref):
    cross = joint_ref.shape[1]
    pair = picked_ref.shape[1]
    z = lax.dot_general(
        otm_ref[:, :cross], picked_ref[...], TN, preferred_element_type=F32
    )
    keep = lax.broadcasted_iota(jnp.int32, z.shape, 0) < count_ref[0]
    z = jnp.where(keep, z, 0.0).astype(BF16)
    after = lax.dot_general(
        next_otm_ref[...], next_picked_ref[...], TN, preferred_element_type=F32
    ).astype(BF16)
    value = cross_block(z, turned(z), after, 2.0 / pair)
    joint_ref[0] = value[:cross]
    joint_ref[1] = value[cross:]


def per_device(mode_shapes, modal_freq, damping, excitation, modal_load, attach, row_count, otm):
    count = lax.axis_size("mode")
    half = count // 2
    iface, modes = mode_shapes.shape
    rows_max, att = otm.shape[1], otm.shape[2]
    lines = excitation.shape[0]
    width = modal_load.shape[3]
    pair = 2 * width
    columns = lines * pair
    smem = pl.BlockSpec(memory_space=pltpu.SMEM)
    vmem = pl.BlockSpec(memory_space=pltpu.VMEM)
    hbm = pl.BlockSpec(memory_space=pl.ANY)
    load_t = jnp.transpose(modal_load, (1, 2, 3, 0))
    otm_t = jnp.transpose(otm[0], (1, 0))
    part = jax.ShapeDtypeStruct((att, columns), BF16)
    part_wide = jax.ShapeDtypeStruct((att, columns), F32)
    chunks = CHUNKS if iface % (16 * CHUNKS) == 0 else 1
    scratch = [
        pltpu.VMEM((iface, modes), BF16),
        pltpu.VMEM((iface, modes), F32),
        pltpu.VMEM((att, modes), F32),
        pltpu.SemaphoreType.DMA((chunks,)),
    ]
    params = pltpu.CompilerParams(vmem_limit_bytes=40 << 20)
    steps = list(range(1, half))
    far_slots = [half ^ k for k in steps] + [half]
    near_slots = steps + [0]
    *far, far_own, resp = pl.pallas_call(
        functools.partial(far_kernel, far_slots),
        out_shape=[part] * (half - 1)
        + [part_wide, jax.ShapeDtypeStruct((columns, modes), BF16)],
        in_specs=[smem, smem, vmem, vmem, hbm, hbm],
        out_specs=[vmem] * (half + 1),
        scratch_shapes=[pltpu.VMEM(load_t.shape, F32)] + scratch + [pltpu.SemaphoreType.DMA],
        compiler_params=params,
        name="far_parts",
    )(attach, excitation, modal_freq.reshape(1, -1), damping.reshape(1, -1), load_t, mode_shapes)
    *near, near_own = pl.pallas_call(
        functools.partial(near_kernel, near_slots),
        out_shape=[part] * (half - 1) + [part_wide],
        in_specs=[smem, vmem, hbm],
        out_specs=[vmem] * half,
        scratch_shapes=scratch,
        compiler_params=params,
        name="near_parts",
    )(attach, resp, mode_shapes)

    def swapped(value, k):
        return lax.ppermute(value, "mode", [(i, i ^ k) for i in range(count)])

    def following(value):
        return lax.ppermute(value, "mode", [(i, i - 1) for i in range(1, count)])

    far_sum = far_own
    for k, value in zip(steps, far):
        far_sum = far_sum + swapped(value, k).astype(F32)
    picked = near_own
    for k, value in zip(steps, near):
        picked = picked + swapped(value, k).astype(F32)
    picked = picked + swapped(far_sum.astype(BF16), half).astype(F32)
    picked = picked.astype(BF16)

    keep = jnp.arange(rows_max, dtype=jnp.int32)[None, :] < row_count[:, None]
    next_otm = following(jnp.where(keep, otm_t, jnp.zeros_like(otm_t)))
    next_picked = following(picked)

    columns_of = pl.BlockSpec((att, pair), lambda f: (0, f))
    whole = pl.BlockSpec((att, rows_max), lambda f: (0, 0))
    csd = pl.pallas_call(
        auto_kernel,
        grid=(lines,),
        out_shape=jax.ShapeDtypeStruct((1, lines, 2, rows_max, rows_max), BF16),
        in_specs=[smem, whole, columns_of],
        out_specs=pl.BlockSpec((None, None, 2, rows_max, rows_max), lambda f: (0, f, 0, 0, 0)),
        name="auto_csd",
    )(row_count, otm_t, picked)
    joint = pl.pallas_call(
        joint_kernel,
        grid=(lines,),
        out_shape=jax.ShapeDtypeStruct((1, lines, 2, CROSS, rows_max), BF16),
        in_specs=[smem, whole, columns_of, whole, columns_of],
        out_specs=pl.BlockSpec((None, None, 2, CROSS, rows_max), lambda f: (0, f, 0, 0, 0)),
        name="joint_csd",
    )(row_count, otm_t, picked, next_otm, next_picked)
    return (csd, joint)


def solution(mesh):
    return jax.shard_map(
        per_device,
        mesh=mesh,
        in_specs=(
            P(None, "mode"),
            P("mode"),
            P("mode"),
            P("freq"),
            P("mode", "freq", None, None),
            P(),
            P("mode"),
            P("mode", None, None),
        ),
        out_specs=(P("mode", "freq", None, None, None), P("mode", "freq", None, None, None)),
        check_vma=False,
    )
```

```python
import functools

import jax
import jax.numpy as jnp
from jax import lax
from jax.experimental import pallas as pl
from jax.experimental.pallas import tpu as pltpu
from jax.sharding import PartitionSpec as P

CROSS = 128
CHUNKS = 6
LANES = 128
F32 = jnp.float32
BF16 = jnp.bfloat16
NT = (((1,), (1,)), ((), ()))
TN = (((0,), (0,)), ((), ()))


def modal_response(freq_ref, damp_ref, exc_ref, load_ref, resp_ref):
    lines = load_ref.shape[0]
    width = load_ref.shape[2]
    freq = freq_ref[...].reshape(1, -1)
    damp = damp_ref[...].reshape(1, -1)
    omega_sq = freq * freq
    for f in range(lines):
        exc = exc_ref[f]
        a = omega_sq - exc * exc
        b = 2.0 * damp * freq * exc
        denom = a * a + b * b
        frf_re = omega_sq * a / denom
        frf_im = -omega_sq * b / denom
        load_re = load_ref[f, 0]
        load_im = load_ref[f, 1]
        base = f * 2 * width
        resp_ref[base : base + width, :] = (frf_re * load_re - frf_im * load_im).astype(BF16)
        resp_ref[base + width : base + 2 * width, :] = (
            frf_re * load_im + frf_im * load_re
        ).astype(BF16)


def parts_kernel(
    slots, attach_hbm, exc_hbm, count_hbm, freq_hbm, damp_hbm, load_hbm, otm_hbm, shapes_hbm, *rest
):
    outs = rest[: len(slots)]
    otm_ref = rest[len(slots)]
    (attach, exc, rows_here, freq, damp, load, otm, raw, wide, picks, resp, sems, small) = rest[
        len(slots) + 1 :
    ]
    copies = [
        pltpu.make_async_copy(source, target, small.at[i])
        for i, (source, target) in enumerate(
            [
                (freq_hbm, freq),
                (damp_hbm, damp),
                (exc_hbm, exc),
                (load_hbm, load),
                (attach_hbm, attach),
                (count_hbm, rows_here),
                (otm_hbm, otm),
            ]
        )
    ]
    for copy in copies:
        copy.start()
    chunks = sems.shape[0]
    step = raw.shape[0] // chunks
    pieces = raw.shape[1] // LANES
    att = picks.shape[0] // (len(slots) * pieces)

    def fetch(i):
        rows = pl.ds(pl.multiple_of(i * step, step), step)
        return pltpu.make_async_copy(shapes_hbm.at[rows, :], raw.at[rows, :], sems.at[i])

    for i in range(chunks):
        fetch(i).start()
    for copy in copies:
        copy.wait()
    modal_response(freq, damp, exc, load, resp)
    lane = lax.broadcasted_iota(jnp.int32, otm.shape, 1)
    otm_ref[...] = jnp.where(lane < rows_here[0], otm[...], jnp.zeros_like(otm))

    def widen(i, carry):
        fetch(i).wait()
        first = pl.multiple_of(i * step, step)
        for k in range(pieces):
            block = raw[pl.ds(first, step), k * LANES : (k + 1) * LANES]
            wide[pl.ds(first * pieces + k, step, stride=pieces), :] = block.astype(F32)
        return carry

    lax.fori_loop(0, chunks, widen, 0)
    me = lax.axis_index("mode")

    def pick(slot, first):
        comp = jnp.bitwise_xor(me, slot)
        rows = [wide[pl.ds(attach[comp, a] * pieces, pieces), :] for a in range(att)]
        for a in range(att):
            picks[pl.ds(first + a * pieces, pieces), :] = rows[a]

    for i, slot in enumerate(slots):
        pick(slot, i * att * pieces)
    group = min(8, len(slots))
    for start in range(0, len(slots), group):
        count = group * att
        lhs = jnp.concatenate(
            [
                picks[pl.ds(start * att * pieces + k, count, stride=pieces), :].astype(BF16)
                for k in range(pieces)
            ],
            axis=1,
        )
        part = lax.dot_general(lhs, resp[...], NT, preferred_element_type=F32)
        for i in range(group):
            out = outs[start + i]
            out[...] = part[i * att : (i + 1) * att].astype(out.dtype)


def turned(z):
    width = z.shape[1] // 2
    return jnp.concatenate([z[:, width:], -z[:, :width]], axis=1)


def spectra(left, right, out_hbm, buffer, sems, f):
    pair = left.shape[1]
    rows = left.shape[0]
    both = jnp.concatenate([left, turned(left)], axis=0)
    value = lax.dot_general(both, right, NT, preferred_element_type=F32) * (2.0 / pair)
    value = value.astype(BF16)
    buffer[f, 0] = value[:rows]
    buffer[f, 1] = value[rows:]
    copy = pltpu.make_async_copy(buffer.at[f], out_hbm.at[0, f], sems.at[f])
    copy.start()
    return copy


def auto_kernel(otm_ref, picked_ref, csd_hbm, left_ref, buffer, sems):
    lines = buffer.shape[0]
    cross = left_ref.shape[0]
    z = lax.dot_general(otm_ref[...], picked_ref[...], TN, preferred_element_type=F32)
    z = z.astype(BF16)
    pair = z.shape[1] // lines
    left_ref[...] = z[:cross]
    copies = []
    for f in range(lines):
        line = z[:, f * pair : (f + 1) * pair]
        copies.append(spectra(line, line, csd_hbm, buffer, sems, f))
    for copy in copies:
        copy.wait()


def joint_kernel(left_ref, otm_ref, picked_ref, joint_hbm, buffer, sems):
    lines = buffer.shape[0]
    z = lax.dot_general(otm_ref[...], picked_ref[...], TN, preferred_element_type=F32)
    z = z.astype(BF16)
    pair = z.shape[1] // lines
    copies = []
    for f in range(lines):
        columns = slice(f * pair, (f + 1) * pair)
        copies.append(
            spectra(left_ref[:, columns], z[:, columns], joint_hbm, buffer, sems, f)
        )
    for copy in copies:
        copy.wait()


def per_device(mode_shapes, modal_freq, damping, excitation, modal_load, attach, row_count, otm):
    count = lax.axis_size("mode")
    half = count // 2
    iface, modes = mode_shapes.shape
    rows_max, att = otm.shape[1], otm.shape[2]
    lines = excitation.shape[0]
    pair = 2 * modal_load.shape[3]
    columns = lines * pair
    vmem = pl.BlockSpec(memory_space=pltpu.VMEM)
    hbm = pl.BlockSpec(memory_space=pl.ANY)
    load_t = jnp.transpose(modal_load, (1, 2, 3, 0))
    otm_t = jnp.transpose(otm[0], (1, 0))
    part = jax.ShapeDtypeStruct((att, columns), BF16)
    part_wide = jax.ShapeDtypeStruct((att, columns), F32)
    chunks = CHUNKS if iface % (16 * CHUNKS) == 0 else 1
    pieces = modes // LANES
    steps = list(range(1, half))
    slots = [half ^ k for k in steps] + [half] + steps + [0]
    outs = pl.pallas_call(
        functools.partial(parts_kernel, slots),
        out_shape=([part] * (half - 1) + [part_wide]) * 2
        + [jax.ShapeDtypeStruct(otm_t.shape, BF16)],
        in_specs=[hbm] * 8,
        out_specs=[vmem] * (count + 1),
        scratch_shapes=[
            pltpu.SMEM(attach.shape, jnp.int32),
            pltpu.SMEM(excitation.shape, F32),
            pltpu.SMEM(row_count.shape, jnp.int32),
            pltpu.VMEM(modal_freq.shape, F32),
            pltpu.VMEM(damping.shape, F32),
            pltpu.VMEM(load_t.shape, F32),
            pltpu.VMEM(otm_t.shape, BF16),
            pltpu.VMEM((iface, modes), BF16),
            pltpu.VMEM((iface * pieces, LANES), F32),
            pltpu.VMEM((count * att * pieces, LANES), F32),
            pltpu.VMEM((columns, modes), BF16),
            pltpu.SemaphoreType.DMA((chunks,)),
            pltpu.SemaphoreType.DMA((7,)),
        ],
        compiler_params=pltpu.CompilerParams(vmem_limit_bytes=60 << 20),
        name="partial_sums",
    )(attach, excitation, row_count, modal_freq, damping, load_t, otm_t, mode_shapes)
    far, far_own = outs[: half - 1], outs[half - 1]
    near, near_own = outs[half : count - 1], outs[count - 1]
    own_otm = outs[count]

    def swapped(value, k):
        return lax.ppermute(value, "mode", [(i, i ^ k) for i in range(count)])

    def following(value):
        return lax.ppermute(value, "mode", [(i, i - 1) for i in range(1, count)])

    far_sum = far_own
    for k, value in zip(steps, far):
        far_sum = far_sum + swapped(value, k).astype(F32)
    picked = near_own
    for k, value in zip(steps, near):
        picked = picked + swapped(value, k).astype(F32)
    picked = picked + swapped(far_sum.astype(BF16), half).astype(F32)
    picked = picked.astype(BF16)
    next_otm = following(own_otm)
    next_picked = following(picked)

    params = pltpu.CompilerParams(vmem_limit_bytes=24 << 20)
    csd, left = pl.pallas_call(
        auto_kernel,
        out_shape=[
            jax.ShapeDtypeStruct((1, lines, 2, rows_max, rows_max), BF16),
            jax.ShapeDtypeStruct((CROSS, columns), BF16),
        ],
        in_specs=[vmem] * 2,
        out_specs=[hbm, vmem],
        scratch_shapes=[
            pltpu.VMEM((lines, 2, rows_max, rows_max), BF16),
            pltpu.SemaphoreType.DMA((lines,)),
        ],
        compiler_params=params,
        name="auto_csd",
    )(own_otm, picked)
    joint = pl.pallas_call(
        joint_kernel,
        out_shape=jax.ShapeDtypeStruct((1, lines, 2, CROSS, rows_max), BF16),
        in_specs=[vmem] * 3,
        out_specs=hbm,
        scratch_shapes=[
            pltpu.VMEM((lines, 2, CROSS, rows_max), BF16),
            pltpu.SemaphoreType.DMA((lines,)),
        ],
        compiler_params=params,
        name="joint_csd",
    )(left, next_otm, next_picked)
    return (csd, joint)


def solution(mesh):
    return jax.shard_map(
        per_device,
        mesh=mesh,
        in_specs=(
            P(None, "mode"),
            P("mode"),
            P("mode"),
            P("freq"),
            P("mode", "freq", None, None),
            P(),
            P("mode"),
            P("mode", None, None),
        ),
        out_specs=(P("mode", "freq", None, None, None), P("mode", "freq", None, None, None)),
        check_vma=False,
    )
```

```python
import functools

import jax
import jax.numpy as jnp
from jax import lax
from jax.experimental import pallas as pl
from jax.experimental.pallas import tpu as pltpu
from jax.sharding import PartitionSpec as P

CROSS = 128
CHUNKS = 6
LANES = 128
F32 = jnp.float32
BF16 = jnp.bfloat16
NT = (((1,), (1,)), ((), ()))
TN = (((0,), (0,)), ((), ()))


def modal_response(freq_ref, damp_ref, exc_ref, load_ref, resp_ref):
    lines = load_ref.shape[0]
    width = load_ref.shape[2]
    freq = freq_ref[...].reshape(1, -1)
    damp = damp_ref[...].reshape(1, -1)
    omega_sq = freq * freq
    for f in range(lines):
        exc = exc_ref[f]
        a = omega_sq - exc * exc
        b = 2.0 * damp * freq * exc
        denom = a * a + b * b
        frf_re = omega_sq * a / denom
        frf_im = -omega_sq * b / denom
        load_re = load_ref[f, 0]
        load_im = load_ref[f, 1]
        base = f * 2 * width
        resp_ref[base : base + width, :] = (frf_re * load_re - frf_im * load_im).astype(BF16)
        resp_ref[base + width : base + 2 * width, :] = (
            frf_re * load_im + frf_im * load_re
        ).astype(BF16)


def parts_kernel(
    slots, attach_hbm, exc_hbm, freq_hbm, damp_hbm, load_hbm, shapes_hbm, *rest
):
    outs = rest[: len(slots)]
    attach, exc, freq, damp, load, raw, wide, picks, resp, sems, small = rest[len(slots) :]
    copies = [
        pltpu.make_async_copy(source, target, small.at[i])
        for i, (source, target) in enumerate(
            [
                (freq_hbm, freq),
                (damp_hbm, damp),
                (exc_hbm, exc),
                (load_hbm, load),
                (attach_hbm, attach),
            ]
        )
    ]
    for copy in copies:
        copy.start()
    chunks = sems.shape[0]
    step = raw.shape[0] // chunks
    pieces = raw.shape[1] // LANES
    att = picks.shape[0] // (len(slots) * pieces)

    def fetch(i):
        rows = pl.ds(pl.multiple_of(i * step, step), step)
        return pltpu.make_async_copy(shapes_hbm.at[rows, :], raw.at[rows, :], sems.at[i])

    for i in range(chunks):
        fetch(i).start()
    for copy in copies:
        copy.wait()
    modal_response(freq, damp, exc, load, resp)

    def widen(i, carry):
        fetch(i).wait()
        first = pl.multiple_of(i * step, step)
        for k in range(pieces):
            block = raw[pl.ds(first, step), k * LANES : (k + 1) * LANES]
            wide[pl.ds(first * pieces + k, step, stride=pieces), :] = block.astype(F32)
        return carry

    lax.fori_loop(0, chunks, widen, 0)
    me = lax.axis_index("mode")

    def pick(slot, first):
        comp = jnp.bitwise_xor(me, slot)
        rows = [wide[pl.ds(attach[comp, a] * pieces, pieces), :] for a in range(att)]
        for a in range(att):
            picks[pl.ds(first + a * pieces, pieces), :] = rows[a]

    for i, slot in enumerate(slots):
        pick(slot, i * att * pieces)
    group = min(8, len(slots))
    for start in range(0, len(slots), group):
        count = group * att
        lhs = jnp.concatenate(
            [
                picks[pl.ds(start * att * pieces + k, count, stride=pieces), :].astype(BF16)
                for k in range(pieces)
            ],
            axis=1,
        )
        part = lax.dot_general(lhs, resp[...], NT, preferred_element_type=F32)
        for i in range(group):
            out = outs[start + i]
            out[...] = part[i * att : (i + 1) * att].astype(out.dtype)


def turned(z):
    width = z.shape[1] // 2
    return jnp.concatenate([z[:, width:], -z[:, :width]], axis=1)


def spectra(left, right, out_hbm, buffer, sems, f):
    pair = left.shape[1]
    rows = left.shape[0]
    both = jnp.concatenate([left, turned(left)], axis=0)
    value = lax.dot_general(both, right, NT, preferred_element_type=F32) * (2.0 / pair)
    value = value.astype(BF16)
    buffer[f, 0] = value[:rows]
    buffer[f, 1] = value[rows:]
    copy = pltpu.make_async_copy(buffer.at[f], out_hbm.at[0, f], sems.at[f])
    copy.start()
    return copy


def auto_kernel(otm_ref, picked_ref, csd_hbm, left_ref, buffer, sems):
    lines = buffer.shape[0]
    cross = left_ref.shape[0]
    z = lax.dot_general(otm_ref[...], picked_ref[...], TN, preferred_element_type=F32)
    z = z.astype(BF16)
    pair = z.shape[1] // lines
    left_ref[...] = z[:cross]
    copies = []
    for f in range(lines):
        line = z[:, f * pair : (f + 1) * pair]
        copies.append(spectra(line, line, csd_hbm, buffer, sems, f))
    for copy in copies:
        copy.wait()


def joint_kernel(left_ref, otm_ref, picked_ref, joint_hbm, buffer, sems):
    lines = buffer.shape[0]
    z = lax.dot_general(otm_ref[...], picked_ref[...], TN, preferred_element_type=F32)
    z = z.astype(BF16)
    pair = z.shape[1] // lines
    copies = []
    for f in range(lines):
        columns = slice(f * pair, (f + 1) * pair)
        copies.append(
            spectra(left_ref[:, columns], z[:, columns], joint_hbm, buffer, sems, f)
        )
    for copy in copies:
        copy.wait()


def per_device(mode_shapes, modal_freq, damping, excitation, modal_load, attach, row_count, otm):
    count = lax.axis_size("mode")
    half = count // 2
    iface, modes = mode_shapes.shape
    rows_max, att = otm.shape[1], otm.shape[2]
    lines = excitation.shape[0]
    pair = 2 * modal_load.shape[3]
    columns = lines * pair
    vmem = pl.BlockSpec(memory_space=pltpu.VMEM)
    hbm = pl.BlockSpec(memory_space=pl.ANY)
    load_t = jnp.transpose(modal_load, (1, 2, 3, 0))
    otm_t = jnp.transpose(otm[0], (1, 0))
    part = pltpu.VMEM((att, columns), BF16)
    part_wide = pltpu.VMEM((att, columns), F32)
    chunks = CHUNKS if iface % (16 * CHUNKS) == 0 else 1
    pieces = modes // LANES
    steps = list(range(half - 1, 0, -1))
    slots = [half ^ k for k in steps] + [half] + steps + [0]
    outs = pl.pallas_call(
        functools.partial(parts_kernel, slots),
        out_shape=([part] * (half - 1) + [part_wide]) * 2,
        in_specs=[hbm] * 6,
        out_specs=[vmem] * count,
        scratch_shapes=[
            pltpu.SMEM(attach.shape, jnp.int32),
            pltpu.SMEM(excitation.shape, F32),
            pltpu.VMEM(modal_freq.shape, F32),
            pltpu.VMEM(damping.shape, F32),
            pltpu.VMEM(load_t.shape, F32),
            pltpu.VMEM((iface, modes), BF16),
            pltpu.VMEM((iface * pieces, LANES), F32),
            pltpu.VMEM((count * att * pieces, LANES), F32),
            pltpu.VMEM((columns, modes), BF16),
            pltpu.SemaphoreType.DMA((chunks,)),
            pltpu.SemaphoreType.DMA((5,)),
        ],
        compiler_params=pltpu.CompilerParams(vmem_limit_bytes=58 << 20),
        name="partial_sums",
    )(attach, excitation, modal_freq, damping, load_t, mode_shapes)
    far, far_own = list(outs[: half - 1]), outs[half - 1]
    near, near_own = list(outs[half : count - 1]), outs[count - 1]
    used = jnp.arange(rows_max, dtype=jnp.int32)[None, :] < row_count[:, None]
    own_otm = jnp.where(used, otm_t, jnp.zeros_like(otm_t))

    def swapped(value, k):
        return lax.ppermute(value, "mode", [(i, i ^ k) for i in range(count)])

    def following(value):
        return lax.ppermute(value, "mode", [(i, i - 1) for i in range(1, count)])

    far_sum = far_own
    for k, value in zip(steps, far):
        far_sum = far_sum + swapped(value, k).astype(F32)
    next_otm = following(own_otm)
    picked = near_own
    for k, value in zip(steps, near):
        picked = picked + swapped(value, k).astype(F32)
    across = swapped(far_sum.astype(BF16), half)
    picked, next_otm = lax.optimization_barrier((picked, next_otm))
    picked = (picked + across.astype(F32)).astype(BF16)
    next_picked = following(picked)

    params = pltpu.CompilerParams(vmem_limit_bytes=24 << 20)
    csd, left = pl.pallas_call(
        auto_kernel,
        out_shape=[
            jax.ShapeDtypeStruct((1, lines, 2, rows_max, rows_max), BF16),
            jax.ShapeDtypeStruct((CROSS, columns), BF16),
        ],
        in_specs=[vmem] * 2,
        out_specs=[hbm, vmem],
        scratch_shapes=[
            pltpu.VMEM((lines, 2, rows_max, rows_max), BF16),
            pltpu.SemaphoreType.DMA((lines,)),
        ],
        compiler_params=params,
        name="auto_csd",
    )(own_otm, picked)
    joint = pl.pallas_call(
        joint_kernel,
        out_shape=jax.ShapeDtypeStruct((1, lines, 2, CROSS, rows_max), BF16),
        in_specs=[vmem] * 3,
        out_specs=hbm,
        scratch_shapes=[
            pltpu.VMEM((lines, 2, CROSS, rows_max), BF16),
            pltpu.SemaphoreType.DMA((lines,)),
        ],
        compiler_params=params,
        name="joint_csd",
    )(left, next_otm, next_picked)
    return (csd, joint)


def solution(mesh):
    return jax.shard_map(
        per_device,
        mesh=mesh,
        in_specs=(
            P(None, "mode"),
            P("mode"),
            P("mode"),
            P("freq"),
            P("mode", "freq", None, None),
            P(),
            P("mode"),
            P("mode", None, None),
        ),
        out_specs=(P("mode", "freq", None, None, None), P("mode", "freq", None, None, None)),
        check_vma=False,
    )
```

```python
import functools

import jax
import jax.numpy as jnp
from jax import lax
from jax.experimental import pallas as pl
from jax.experimental.pallas import tpu as pltpu
from jax.sharding import PartitionSpec as P

CROSS = 128
CHUNKS = 6
LANES = 128
F32 = jnp.float32
BF16 = jnp.bfloat16
NT = (((1,), (1,)), ((), ()))
TN = (((0,), (0,)), ((), ()))


def modal_response(freq_ref, damp_ref, exc_ref, load_ref, resp_ref):
    lines = load_ref.shape[0]
    width = load_ref.shape[2]
    freq = freq_ref[...].reshape(1, -1)
    damp = damp_ref[...].reshape(1, -1)
    omega_sq = freq * freq
    for f in range(lines):
        exc = exc_ref[f]
        a = omega_sq - exc * exc
        b = 2.0 * damp * freq * exc
        denom = a * a + b * b
        frf_re = omega_sq * a / denom
        frf_im = -omega_sq * b / denom
        load_re = load_ref[f, 0]
        load_im = load_ref[f, 1]
        base = f * 2 * width
        resp_ref[base : base + width, :] = (frf_re * load_re - frf_im * load_im).astype(BF16)
        resp_ref[base + width : base + 2 * width, :] = (
            frf_re * load_im + frf_im * load_re
        ).astype(BF16)


def parts_kernel(
    slots, attach_hbm, exc_hbm, freq_hbm, damp_hbm, load_hbm, shapes_hbm, *rest
):
    outs = rest[: len(slots)]
    attach, exc, freq, damp, load, raw, wide, picks, resp, sems, small = rest[len(slots) :]
    copies = [
        pltpu.make_async_copy(source, target, small.at[i])
        for i, (source, target) in enumerate(
            [
                (freq_hbm, freq),
                (damp_hbm, damp),
                (exc_hbm, exc),
                (load_hbm, load),
                (attach_hbm, attach),
            ]
        )
    ]
    for copy in copies:
        copy.start()
    chunks = sems.shape[0]
    step = raw.shape[0] // chunks
    pieces = raw.shape[1] // LANES
    att = picks.shape[0] // (len(slots) * pieces)

    def fetch(i):
        rows = pl.ds(pl.multiple_of(i * step, step), step)
        return pltpu.make_async_copy(shapes_hbm.at[rows, :], raw.at[rows, :], sems.at[i])

    for i in range(chunks):
        fetch(i).start()
    for copy in copies:
        copy.wait()
    modal_response(freq, damp, exc, load, resp)

    def widen(i, carry):
        fetch(i).wait()
        first = pl.multiple_of(i * step, step)
        for k in range(pieces):
            block = raw[pl.ds(first, step), k * LANES : (k + 1) * LANES]
            wide[pl.ds(first * pieces + k, step, stride=pieces), :] = block.astype(F32)
        return carry

    lax.fori_loop(0, chunks, widen, 0)
    me = lax.axis_index("mode")

    def pick(slot, first):
        comp = jnp.bitwise_xor(me, slot)
        rows = [wide[pl.ds(attach[comp, a] * pieces, pieces), :] for a in range(att)]
        for a in range(att):
            picks[pl.ds(first + a * pieces, pieces), :] = rows[a]

    for i, slot in enumerate(slots):
        pick(slot, i * att * pieces)
    group = min(8, len(slots))
    for start in range(0, len(slots), group):
        count = group * att
        lhs = jnp.concatenate(
            [
                picks[pl.ds(start * att * pieces + k, count, stride=pieces), :].astype(BF16)
                for k in range(pieces)
            ],
            axis=1,
        )
        part = lax.dot_general(lhs, resp[...], NT, preferred_element_type=F32)
        for i in range(group):
            out = outs[start + i]
            out[...] = part[i * att : (i + 1) * att].astype(out.dtype)


def turned(z):
    width = z.shape[1] // 2
    return jnp.concatenate([z[:, width:], -z[:, :width]], axis=1)


def spectra(left, right, out_hbm, buffer, sems, f):
    pair = left.shape[1]
    rows = left.shape[0]
    both = jnp.concatenate([left, turned(left)], axis=0)
    value = lax.dot_general(both, right, NT, preferred_element_type=F32) * (2.0 / pair)
    value = value.astype(BF16)
    buffer[f, 0] = value[:rows]
    buffer[f, 1] = value[rows:]
    copy = pltpu.make_async_copy(buffer.at[f], out_hbm.at[0, f], sems.at[f])
    copy.start()
    return copy


def auto_kernel(otm_ref, picked_ref, csd_hbm, left_ref, buffer, sems):
    lines = buffer.shape[0]
    cross = left_ref.shape[0]
    z = lax.dot_general(otm_ref[...], picked_ref[...], TN, preferred_element_type=F32)
    z = z.astype(BF16)
    pair = z.shape[1] // lines
    left_ref[...] = z[:cross]
    copies = []
    for f in range(lines):
        line = z[:, f * pair : (f + 1) * pair]
        copies.append(spectra(line, line, csd_hbm, buffer, sems, f))
    for copy in copies:
        copy.wait()


def joint_kernel(left_ref, joined_ref, joint_hbm, buffer, sems):
    lines = buffer.shape[0]
    columns = left_ref.shape[1]
    z = lax.dot_general(
        joined_ref[:, columns:], joined_ref[:, :columns], TN, preferred_element_type=F32
    )
    z = z.astype(BF16)
    pair = columns // lines
    copies = []
    for f in range(lines):
        columns = slice(f * pair, (f + 1) * pair)
        copies.append(
            spectra(left_ref[:, columns], z[:, columns], joint_hbm, buffer, sems, f)
        )
    for copy in copies:
        copy.wait()


def per_device(mode_shapes, modal_freq, damping, excitation, modal_load, attach, row_count, otm):
    count = lax.axis_size("mode")
    half = count // 2
    iface, modes = mode_shapes.shape
    rows_max, att = otm.shape[1], otm.shape[2]
    lines = excitation.shape[0]
    pair = 2 * modal_load.shape[3]
    columns = lines * pair
    vmem = pl.BlockSpec(memory_space=pltpu.VMEM)
    hbm = pl.BlockSpec(memory_space=pl.ANY)
    load_t = jnp.transpose(modal_load, (1, 2, 3, 0))
    otm_t = jnp.transpose(otm[0], (1, 0))
    part = pltpu.VMEM((att, columns), BF16)
    part_wide = pltpu.VMEM((att, columns), F32)
    chunks = CHUNKS if iface % (16 * CHUNKS) == 0 else 1
    pieces = modes // LANES
    steps = list(range(half - 1, 0, -1))
    slots = [half ^ k for k in steps] + [half] + steps + [0]
    outs = pl.pallas_call(
        functools.partial(parts_kernel, slots),
        out_shape=([part] * (half - 1) + [part_wide]) * 2,
        in_specs=[hbm] * 6,
        out_specs=[vmem] * count,
        scratch_shapes=[
            pltpu.SMEM(attach.shape, jnp.int32),
            pltpu.SMEM(excitation.shape, F32),
            pltpu.VMEM(modal_freq.shape, F32),
            pltpu.VMEM(damping.shape, F32),
            pltpu.VMEM(load_t.shape, F32),
            pltpu.VMEM((iface, modes), BF16),
            pltpu.VMEM((iface * pieces, LANES), F32),
            pltpu.VMEM((count * att * pieces, LANES), F32),
            pltpu.VMEM((columns, modes), BF16),
            pltpu.SemaphoreType.DMA((chunks,)),
            pltpu.SemaphoreType.DMA((5,)),
        ],
        compiler_params=pltpu.CompilerParams(vmem_limit_bytes=58 << 20),
        name="partial_sums",
    )(attach, excitation, modal_freq, damping, load_t, mode_shapes)
    far, far_own = list(outs[: half - 1]), outs[half - 1]
    near, near_own = list(outs[half : count - 1]), outs[count - 1]
    used = jnp.arange(rows_max, dtype=jnp.int32)[None, :] < row_count[:, None]
    own_otm = jnp.where(used, otm_t, jnp.zeros_like(otm_t))

    def swapped(value, k):
        return lax.ppermute(value, "mode", [(i, i ^ k) for i in range(count)])

    def following(value):
        return lax.ppermute(value, "mode", [(i, i - 1) for i in range(1, count)])

    far_sum = far_own
    for k, value in zip(steps, far):
        far_sum = far_sum + swapped(value, k).astype(F32)
    picked = near_own
    for k, value in zip(steps, near):
        picked = picked + swapped(value, k).astype(F32)
    far_sum, own_otm = lax.optimization_barrier((far_sum.astype(BF16), own_otm))
    picked = picked + swapped(far_sum, half).astype(F32)
    picked = picked.astype(BF16)
    joined = following(jnp.concatenate([picked, own_otm], axis=1))

    params = pltpu.CompilerParams(vmem_limit_bytes=24 << 20)
    csd, left = pl.pallas_call(
        auto_kernel,
        out_shape=[
            jax.ShapeDtypeStruct((1, lines, 2, rows_max, rows_max), BF16),
            jax.ShapeDtypeStruct((CROSS, columns), BF16),
        ],
        in_specs=[vmem] * 2,
        out_specs=[hbm, vmem],
        scratch_shapes=[
            pltpu.VMEM((lines, 2, rows_max, rows_max), BF16),
            pltpu.SemaphoreType.DMA((lines,)),
        ],
        compiler_params=params,
        name="auto_csd",
    )(own_otm, picked)
    joint = pl.pallas_call(
        joint_kernel,
        out_shape=jax.ShapeDtypeStruct((1, lines, 2, CROSS, rows_max), BF16),
        in_specs=[vmem] * 2,
        out_specs=hbm,
        scratch_shapes=[
            pltpu.VMEM((lines, 2, CROSS, rows_max), BF16),
            pltpu.SemaphoreType.DMA((lines,)),
        ],
        compiler_params=params,
        name="joint_csd",
    )(left, joined)
    return (csd, joint)


def solution(mesh):
    return jax.shard_map(
        per_device,
        mesh=mesh,
        in_specs=(
            P(None, "mode"),
            P("mode"),
            P("mode"),
            P("freq"),
            P("mode", "freq", None, None),
            P(),
            P("mode"),
            P("mode", None, None),
        ),
        out_specs=(P("mode", "freq", None, None, None), P("mode", "freq", None, None, None)),
        check_vma=False,
    )
```

```python
import functools

import jax
import jax.numpy as jnp
from jax import lax
from jax.experimental import pallas as pl
from jax.experimental.pallas import tpu as pltpu
from jax.sharding import PartitionSpec as P

CROSS = 128
CHUNKS = 4
LANES = 128
F32 = jnp.float32
BF16 = jnp.bfloat16
NT = (((1,), (1,)), ((), ()))
NN = (((1,), (0,)), ((), ()))
TN = (((0,), (0,)), ((), ()))


def modal_response(freq_ref, damp_ref, exc_ref, load_ref, resp_ref):
    lines = load_ref.shape[0]
    width = load_ref.shape[2]
    freq = freq_ref[...].reshape(1, -1)
    damp = damp_ref[...].reshape(1, -1)
    omega_sq = freq * freq
    for f in range(lines):
        exc = exc_ref[f]
        a = omega_sq - exc * exc
        b = 2.0 * damp * freq * exc
        denom = a * a + b * b
        frf_re = omega_sq * a / denom
        frf_im = -omega_sq * b / denom
        load_re = load_ref[f, 0]
        load_im = load_ref[f, 1]
        base = f * 2 * width
        resp_ref[base : base + width, :] = (frf_re * load_re - frf_im * load_im).astype(BF16)
        resp_ref[base + width : base + 2 * width, :] = (
            frf_re * load_im + frf_im * load_re
        ).astype(BF16)


def parts_kernel(
    slots, attach_hbm, exc_hbm, freq_hbm, damp_hbm, load_hbm, shapes_hbm, *rest
):
    outs = rest[: len(slots)]
    attach, exc, freq, damp, load, raw, wide, picks, resp, sems, small = rest[len(slots) :]
    copies = [
        pltpu.make_async_copy(source, target, small.at[i])
        for i, (source, target) in enumerate(
            [
                (freq_hbm, freq),
                (damp_hbm, damp),
                (exc_hbm, exc),
                (load_hbm, load),
                (attach_hbm, attach),
            ]
        )
    ]
    for copy in copies:
        copy.start()
    chunks = sems.shape[0]
    step = raw.shape[0] // chunks
    pieces = raw.shape[1] // LANES
    att = picks.shape[0] // (len(slots) * pieces)

    def fetch(i):
        rows = pl.ds(pl.multiple_of(i * step, step), step)
        return pltpu.make_async_copy(shapes_hbm.at[rows, :], raw.at[rows, :], sems.at[i])

    for i in range(chunks):
        fetch(i).start(priority=i % 2)
    for copy in copies:
        copy.wait()
    modal_response(freq, damp, exc, load, resp)

    def widen(i, carry):
        fetch(i).wait()
        first = pl.multiple_of(i * step, step)
        for k in range(pieces):
            block = raw[pl.ds(first, step), k * LANES : (k + 1) * LANES]
            wide[pl.ds(first * pieces + k, step, stride=pieces), :] = block.astype(F32)
        return carry

    lax.fori_loop(0, chunks, widen, 0)
    me = lax.axis_index("mode")

    def pick(slot, first):
        comp = jnp.bitwise_xor(me, slot)
        rows = [wide[pl.ds(attach[comp, a] * pieces, pieces), :] for a in range(att)]
        for a in range(att):
            picks[pl.ds(first + a * pieces, pieces), :] = rows[a]

    group = min(4, len(slots))
    for i, slot in enumerate(slots[:group]):
        pick(slot, i * att * pieces)
    for start in range(0, len(slots), group):
        count = group * att
        for i, slot in enumerate(slots[start + group : start + 2 * group]):
            pick(slot, (start + group + i) * att * pieces)
        lhs = jnp.concatenate(
            [
                picks[pl.ds(start * att * pieces + k, count, stride=pieces), :].astype(BF16)
                for k in range(pieces)
            ],
            axis=1,
        )
        part = lax.dot_general(lhs, resp[...], NT, preferred_element_type=F32)
        for i in range(group):
            out = outs[start + i]
            out[...] = part[i * att : (i + 1) * att].astype(out.dtype)


def turned(z):
    width = z.shape[1] // 2
    return jnp.concatenate([z[:, width:], -z[:, :width]], axis=1)


def spectra(both, right, out_hbm, buffer, sems, f, form=NT):
    pair = both.shape[1]
    rows = both.shape[0] // 2
    value = lax.dot_general(both, right, form, preferred_element_type=F32) * (2.0 / pair)
    value = value.astype(BF16)
    buffer[f, 0] = value[:rows]
    buffer[f, 1] = value[rows:]
    copy = pltpu.make_async_copy(buffer.at[f], out_hbm.at[0, f], sems.at[f])
    copy.start()
    return copy


def auto_kernel(otm_ref, picked_ref, csd_hbm, left_ref, buffer, sems):
    lines = buffer.shape[0]
    cross = left_ref.shape[0] // 2
    z = lax.dot_general(otm_ref[...], picked_ref[...], TN, preferred_element_type=F32)
    z = z.astype(BF16)
    pair = z.shape[1] // lines
    copies = []
    for f in range(lines):
        line = z[:, f * pair : (f + 1) * pair]
        left_ref[: cross, f * pair : (f + 1) * pair] = line[:cross]
        left_ref[cross :, f * pair : (f + 1) * pair] = turned(line[:cross])
        copies.append(spectra(jnp.concatenate([line, turned(line)], axis=0), line, csd_hbm, buffer, sems, f))
    for copy in copies:
        copy.wait()


def joint_kernel(left_ref, joined_ref, joint_hbm, buffer, sems):
    lines = buffer.shape[0]
    columns = left_ref.shape[1]
    z = lax.dot_general(
        joined_ref[:, :columns], joined_ref[:, columns:], TN, preferred_element_type=F32
    )
    z = z.astype(BF16)
    pair = columns // lines
    copies = []
    for f in range(lines):
        part = slice(f * pair, (f + 1) * pair)
        copies.append(
            spectra(left_ref[:, part], z[part], joint_hbm, buffer, sems, f, NN)
        )
    for copy in copies:
        copy.wait()


def per_device(mode_shapes, modal_freq, damping, excitation, modal_load, attach, row_count, otm):
    count = lax.axis_size("mode")
    half = count // 2
    iface, modes = mode_shapes.shape
    rows_max, att = otm.shape[1], otm.shape[2]
    lines = excitation.shape[0]
    pair = 2 * modal_load.shape[3]
    columns = lines * pair
    vmem = pl.BlockSpec(memory_space=pltpu.VMEM)
    hbm = pl.BlockSpec(memory_space=pl.ANY)
    load_t = jnp.transpose(modal_load, (1, 2, 3, 0))
    otm_t = jnp.transpose(otm[0], (1, 0))
    part = pltpu.VMEM((att, columns), BF16)
    part_wide = pltpu.VMEM((att, columns), F32)
    chunks = CHUNKS if iface % (16 * CHUNKS) == 0 else 1
    pieces = modes // LANES
    steps = list(range(half - 1, 0, -1))
    slots = [half ^ k for k in steps] + [half] + steps + [0]
    outs = pl.pallas_call(
        functools.partial(parts_kernel, slots),
        out_shape=([part] * (half - 1) + [part_wide]) * 2,
        in_specs=[hbm] * 6,
        out_specs=[vmem] * count,
        scratch_shapes=[
            pltpu.SMEM(attach.shape, jnp.int32),
            pltpu.SMEM(excitation.shape, F32),
            pltpu.VMEM(modal_freq.shape, F32),
            pltpu.VMEM(damping.shape, F32),
            pltpu.VMEM(load_t.shape, F32),
            pltpu.VMEM((iface, modes), BF16),
            pltpu.VMEM((iface * pieces, LANES), F32),
            pltpu.VMEM((count * att * pieces, LANES), F32),
            pltpu.VMEM((columns, modes), BF16),
            pltpu.SemaphoreType.DMA((chunks,)),
            pltpu.SemaphoreType.DMA((5,)),
        ],
        compiler_params=pltpu.CompilerParams(vmem_limit_bytes=58 << 20),
        name="partial_sums",
    )(attach, excitation, modal_freq, damping, load_t, mode_shapes)
    far, far_own = list(outs[: half - 1]), outs[half - 1]
    near, near_own = list(outs[half : count - 1]), outs[count - 1]
    used = jnp.arange(rows_max, dtype=jnp.int32)[None, :] < row_count[:, None]
    own_otm = jnp.where(used, otm_t, jnp.zeros_like(otm_t))

    def swapped(value, k):
        return lax.ppermute(value, "mode", [(i, i ^ k) for i in range(count)])

    def following(value):
        return lax.ppermute(value, "mode", [(i, i - 1) for i in range(1, count)])

    far_sum = far_own
    for k, value in zip(steps, far):
        far_sum = far_sum + swapped(value, k).astype(F32)
    picked = near_own
    for k, value in zip(steps, near):
        picked = picked + swapped(value, k).astype(F32)
    far_sum, own_otm = lax.optimization_barrier((far_sum.astype(BF16), own_otm))
    picked = picked + swapped(far_sum, half).astype(F32)
    picked = picked.astype(BF16)
    joined = following(jnp.concatenate([picked, own_otm], axis=1))

    params = pltpu.CompilerParams(vmem_limit_bytes=24 << 20)
    csd, left = pl.pallas_call(
        auto_kernel,
        out_shape=[
            jax.ShapeDtypeStruct((1, lines, 2, rows_max, rows_max), BF16),
            jax.ShapeDtypeStruct((2 * CROSS, columns), BF16),
        ],
        in_specs=[vmem] * 2,
        out_specs=[hbm, vmem],
        scratch_shapes=[
            pltpu.VMEM((lines, 2, rows_max, rows_max), BF16),
            pltpu.SemaphoreType.DMA((lines,)),
        ],
        compiler_params=params,
        name="auto_csd",
    )(own_otm, picked)
    joint = pl.pallas_call(
        joint_kernel,
        out_shape=jax.ShapeDtypeStruct((1, lines, 2, CROSS, rows_max), BF16),
        in_specs=[vmem] * 2,
        out_specs=hbm,
        scratch_shapes=[
            pltpu.VMEM((lines, 2, CROSS, rows_max), BF16),
            pltpu.SemaphoreType.DMA((lines,)),
        ],
        compiler_params=params,
        name="joint_csd",
    )(left, joined)
    return (csd, joint)


def solution(mesh):
    return jax.shard_map(
        per_device,
        mesh=mesh,
        in_specs=(
            P(None, "mode"),
            P("mode"),
            P("mode"),
            P("freq"),
            P("mode", "freq", None, None),
            P(),
            P("mode"),
            P("mode", None, None),
        ),
        out_specs=(P("mode", "freq", None, None, None), P("mode", "freq", None, None, None)),
        check_vma=False,
    )
```

```python
import functools

import jax
import jax.numpy as jnp
from jax import lax
from jax.experimental import pallas as pl
from jax.experimental.pallas import tpu as pltpu
from jax.sharding import PartitionSpec as P

CROSS = 128
CHUNKS = 4
LANES = 128
SPARE = 8
F32 = jnp.float32
BF16 = jnp.bfloat16
NT = (((1,), (1,)), ((), ()))
NN = (((1,), (0,)), ((), ()))
TN = (((0,), (0,)), ((), ()))


def modal_response(freq_ref, damp_ref, exc_ref, load_ref, resp_ref):
    lines = load_ref.shape[0]
    width = load_ref.shape[2]
    freq = freq_ref[...].reshape(1, -1)
    damp = damp_ref[...].reshape(1, -1)
    omega_sq = freq * freq
    for f in range(lines):
        exc = exc_ref[f]
        a = omega_sq - exc * exc
        b = 2.0 * damp * freq * exc
        denom = a * a + b * b
        frf_re = omega_sq * a / denom
        frf_im = -omega_sq * b / denom
        load_re = load_ref[f, 0]
        load_im = load_ref[f, 1]
        base = f * 2 * width
        resp_ref[base : base + width, :] = (frf_re * load_re - frf_im * load_im).astype(BF16)
        resp_ref[base + width : base + 2 * width, :] = (
            frf_re * load_im + frf_im * load_re
        ).astype(BF16)


def parts_kernel(
    slots, attach_hbm, exc_hbm, freq_hbm, damp_hbm, load_hbm, shapes_hbm, *rest
):
    outs = rest[: len(slots)]
    attach, exc, freq, damp, load, raw, wide, picks, resp, sems, small = rest[len(slots) :]
    copies = [
        pltpu.make_async_copy(source, target, small.at[i])
        for i, (source, target) in enumerate(
            [
                (freq_hbm, freq),
                (damp_hbm, damp),
                (exc_hbm, exc),
                (load_hbm, load),
                (attach_hbm, attach),
            ]
        )
    ]
    for copy in copies:
        copy.start()
    chunks = sems.shape[0]
    step = raw.shape[0] // chunks
    pieces = raw.shape[1] // LANES
    att = attach.shape[1]

    def fetch(i):
        rows = pl.ds(pl.multiple_of(i * step, step), step)
        return pltpu.make_async_copy(shapes_hbm.at[rows, :], raw.at[rows, :], sems.at[i])

    for i in range(chunks):
        fetch(i).start(priority=i % 2)
    for copy in copies:
        copy.wait()
    modal_response(freq, damp, exc, load, resp)

    def widen(i, carry):
        fetch(i).wait()
        first = pl.multiple_of(i * step, step)
        for k in range(pieces):
            block = raw[pl.ds(first, step), k * LANES : (k + 1) * LANES]
            wide[pl.ds(first * pieces + k, step, stride=pieces), :] = block.astype(F32)
        return carry

    lax.fori_loop(0, chunks, widen, 0)
    me = lax.axis_index("mode")

    def pick(slot, first):
        comp = jnp.bitwise_xor(me, slot)
        rows = [wide[pl.ds(attach[comp, a] * pieces, pieces), :] for a in range(att)]
        for a in range(att):
            picks[pl.ds(first + a * pieces, pieces), :] = rows[a]

    group = min(4, len(slots))
    for i, slot in enumerate(slots[:group]):
        pick(slot, i * att * pieces)
    for start in range(0, len(slots), group):
        count = group * att
        for i, slot in enumerate(slots[start + group : start + 2 * group]):
            pick(slot, (start + group + i) * att * pieces)
        lhs = jnp.concatenate(
            [
                picks[pl.ds(start * att * pieces + k, count, stride=pieces), :].astype(BF16)
                for k in range(pieces)
            ],
            axis=1,
        )
        part = lax.dot_general(lhs, resp[...], NT, preferred_element_type=F32)
        for i in range(group):
            out = outs[start + i]
            out[...] = part[i * att : (i + 1) * att].astype(out.dtype)


def turned(z):
    width = z.shape[1] // 2
    return jnp.concatenate([z[:, width:], -z[:, :width]], axis=1)


def spectra(both, right, out_hbm, buffer, sems, f, form=NT):
    pair = both.shape[1]
    rows = both.shape[0] // 2
    value = lax.dot_general(both, right, form, preferred_element_type=F32) * (2.0 / pair)
    value = value.astype(BF16)
    buffer[f, 0] = value[:rows]
    buffer[f, 1] = value[rows:]
    copy = pltpu.make_async_copy(buffer.at[f], out_hbm.at[0, f], sems.at[f])
    copy.start()
    return copy


def auto_kernel(otm_ref, picked_ref, csd_hbm, left_ref, buffer, sems):
    lines = buffer.shape[0]
    cross = left_ref.shape[0] // 2
    z = lax.dot_general(otm_ref[...], picked_ref[...], TN, preferred_element_type=F32)
    z = z.astype(BF16)
    pair = z.shape[1] // lines
    copies = []
    for f in range(lines):
        line = z[:, f * pair : (f + 1) * pair]
        left_ref[: cross, f * pair : (f + 1) * pair] = line[:cross]
        left_ref[cross :, f * pair : (f + 1) * pair] = turned(line[:cross])
        copies.append(spectra(jnp.concatenate([line, turned(line)], axis=0), line, csd_hbm, buffer, sems, f))
    for copy in copies:
        copy.wait()


def joint_kernel(left_ref, joined_ref, joint_hbm, buffer, sems):
    lines = buffer.shape[0]
    columns = left_ref.shape[1]
    z = lax.dot_general(
        joined_ref[:, :columns], joined_ref[:, columns:], TN, preferred_element_type=F32
    )
    z = z.astype(BF16)
    pair = columns // lines
    copies = []
    for f in range(lines):
        part = slice(f * pair, (f + 1) * pair)
        copies.append(
            spectra(left_ref[:, part], z[part], joint_hbm, buffer, sems, f, NN)
        )
    for copy in copies:
        copy.wait()


def per_device(mode_shapes, modal_freq, damping, excitation, modal_load, attach, row_count, otm):
    count = lax.axis_size("mode")
    half = count // 2
    iface, modes = mode_shapes.shape
    rows_max, att = otm.shape[1], otm.shape[2]
    lines = excitation.shape[0]
    pair = 2 * modal_load.shape[3]
    columns = lines * pair
    vmem = pl.BlockSpec(memory_space=pltpu.VMEM)
    hbm = pl.BlockSpec(memory_space=pl.ANY)
    load_t = jnp.transpose(modal_load, (1, 2, 3, 0))
    otm_t = jnp.transpose(otm[0], (1, 0))
    part = pltpu.VMEM((att, columns), BF16)
    part_wide = pltpu.VMEM((att, columns), F32)
    chunks = CHUNKS if iface % (16 * CHUNKS) == 0 else 1
    pieces = modes // LANES
    steps = list(range(half - 1, 0, -1))
    slots = [half ^ k for k in steps] + [half] + steps + [0]
    outs = pl.pallas_call(
        functools.partial(parts_kernel, slots),
        out_shape=([part] * (half - 1) + [part_wide]) * 2,
        in_specs=[hbm] * 6,
        out_specs=[vmem] * count,
        scratch_shapes=[
            pltpu.SMEM(attach.shape, jnp.int32),
            pltpu.SMEM(excitation.shape, F32),
            pltpu.VMEM(modal_freq.shape, F32),
            pltpu.VMEM(damping.shape, F32),
            pltpu.VMEM(load_t.shape, F32),
            pltpu.VMEM((iface, modes), BF16),
            pltpu.VMEM((iface * pieces + SPARE, LANES), F32),
            pltpu.VMEM((count * att * pieces + SPARE, LANES), F32),
            pltpu.VMEM((columns, modes), BF16),
            pltpu.SemaphoreType.DMA((chunks,)),
            pltpu.SemaphoreType.DMA((5,)),
        ],
        compiler_params=pltpu.CompilerParams(vmem_limit_bytes=58 << 20),
        name="partial_sums",
    )(attach, excitation, modal_freq, damping, load_t, mode_shapes)
    far, far_own = list(outs[: half - 1]), outs[half - 1]
    near, near_own = list(outs[half : count - 1]), outs[count - 1]
    used = jnp.arange(rows_max, dtype=jnp.int32)[None, :] < row_count[:, None]
    own_otm = jnp.where(used, otm_t, jnp.zeros_like(otm_t))

    def swapped(value, k):
        return lax.ppermute(value, "mode", [(i, i ^ k) for i in range(count)])

    def following(value):
        return lax.ppermute(value, "mode", [(i, i - 1) for i in range(1, count)])

    far_sum = far_own
    for k, value in zip(steps, far):
        far_sum = far_sum + swapped(value, k).astype(F32)
    picked = near_own
    for k, value in zip(steps, near):
        picked = picked + swapped(value, k).astype(F32)
    far_sum, own_otm = lax.optimization_barrier((far_sum.astype(BF16), own_otm))
    picked = picked + swapped(far_sum, half).astype(F32)
    picked = picked.astype(BF16)
    joined = following(jnp.concatenate([picked, own_otm], axis=1))

    params = pltpu.CompilerParams(vmem_limit_bytes=24 << 20)
    csd, left = pl.pallas_call(
        auto_kernel,
        out_shape=[
            jax.ShapeDtypeStruct((1, lines, 2, rows_max, rows_max), BF16),
            jax.ShapeDtypeStruct((2 * CROSS, columns), BF16),
        ],
        in_specs=[vmem] * 2,
        out_specs=[hbm, vmem],
        scratch_shapes=[
            pltpu.VMEM((lines, 2, rows_max, rows_max), BF16),
            pltpu.SemaphoreType.DMA((lines,)),
        ],
        compiler_params=params,
        name="auto_csd",
    )(own_otm, picked)
    joint = pl.pallas_call(
        joint_kernel,
        out_shape=jax.ShapeDtypeStruct((1, lines, 2, CROSS, rows_max), BF16),
        in_specs=[vmem] * 2,
        out_specs=hbm,
        scratch_shapes=[
            pltpu.VMEM((lines, 2, CROSS, rows_max), BF16),
            pltpu.SemaphoreType.DMA((lines,)),
        ],
        compiler_params=params,
        name="joint_csd",
    )(left, joined)
    return (csd, joint)


def solution(mesh):
    return jax.shard_map(
        per_device,
        mesh=mesh,
        in_specs=(
            P(None, "mode"),
            P("mode"),
            P("mode"),
            P("freq"),
            P("mode", "freq", None, None),
            P(),
            P("mode"),
            P("mode", None, None),
        ),
        out_specs=(P("mode", "freq", None, None, None), P("mode", "freq", None, None, None)),
        check_vma=False,
    )
```

```python
import functools

import jax
import jax.numpy as jnp
from jax import lax
from jax.experimental import pallas as pl
from jax.experimental.pallas import tpu as pltpu
from jax.sharding import PartitionSpec as P

CROSS = 128
CHUNKS = 6
LANES = 128
SPARE = 8
F32 = jnp.float32
BF16 = jnp.bfloat16
NT = (((1,), (1,)), ((), ()))
NN = (((1,), (0,)), ((), ()))
TN = (((0,), (0,)), ((), ()))


def modal_response(freq_ref, damp_ref, exc_ref, load_ref, resp_ref):
    lines = load_ref.shape[0]
    width = load_ref.shape[2]
    freq = freq_ref[...].reshape(1, -1)
    damp = damp_ref[...].reshape(1, -1)
    omega_sq = freq * freq
    for f in range(lines):
        exc = exc_ref[f]
        a = omega_sq - exc * exc
        b = 2.0 * damp * freq * exc
        denom = a * a + b * b
        frf_re = omega_sq * a / denom
        frf_im = -omega_sq * b / denom
        load_re = load_ref[f, 0]
        load_im = load_ref[f, 1]
        base = f * 2 * width
        resp_ref[base : base + width, :] = (frf_re * load_re - frf_im * load_im).astype(BF16)
        resp_ref[base + width : base + 2 * width, :] = (
            frf_re * load_im + frf_im * load_re
        ).astype(BF16)


def parts_kernel(
    slots, attach_hbm, exc_hbm, freq_hbm, damp_hbm, load_hbm, shapes_hbm, *rest
):
    outs = rest[: len(slots)]
    attach, exc, freq, damp, load, raw, wide, picks, resp, sems, small = rest[len(slots) :]
    copies = [
        pltpu.make_async_copy(source, target, small.at[i])
        for i, (source, target) in enumerate(
            [
                (freq_hbm, freq),
                (damp_hbm, damp),
                (exc_hbm, exc),
                (load_hbm, load),
                (attach_hbm, attach),
            ]
        )
    ]
    for copy in copies:
        copy.start()
    chunks = sems.shape[0]
    step = raw.shape[0] // chunks
    pieces = raw.shape[1] // LANES
    att = attach.shape[1]

    def fetch(i):
        rows = pl.ds(pl.multiple_of(i * step, step), step)
        return pltpu.make_async_copy(shapes_hbm.at[rows, :], raw.at[rows, :], sems.at[i])

    for i in range(chunks):
        fetch(i).start(priority=i % 2)
    for copy in copies:
        copy.wait()
    modal_response(freq, damp, exc, load, resp)

    def widen(i, carry):
        fetch(i).wait()
        first = pl.multiple_of(i * step, step)
        for k in range(pieces):
            block = raw[pl.ds(first, step), k * LANES : (k + 1) * LANES]
            wide[pl.ds(first * pieces + k, step, stride=pieces), :] = block.astype(F32)
        return carry

    lax.fori_loop(0, chunks, widen, 0)
    me = lax.axis_index("mode")

    def pick(slot, first):
        comp = jnp.bitwise_xor(me, slot)
        rows = [wide[pl.ds(attach[comp, a] * pieces, pieces), :] for a in range(att)]
        for a in range(att):
            picks[pl.ds(first + a * pieces, pieces), :] = rows[a]

    group = min(4, len(slots))
    for i, slot in enumerate(slots[:group]):
        pick(slot, i * att * pieces)
    for start in range(0, len(slots), group):
        count = group * att
        for i, slot in enumerate(slots[start + group : start + 2 * group]):
            pick(slot, (start + group + i) * att * pieces)
        lhs = jnp.concatenate(
            [
                picks[pl.ds(start * att * pieces + k, count, stride=pieces), :].astype(BF16)
                for k in range(pieces)
            ],
            axis=1,
        )
        part = lax.dot_general(lhs, resp[...], NT, preferred_element_type=F32)
        for i in range(group):
            out = outs[start + i]
            out[...] = part[i * att : (i + 1) * att].astype(out.dtype)


def turned(z):
    width = z.shape[1] // 2
    return jnp.concatenate([z[:, width:], -z[:, :width]], axis=1)


def spectra(both, right, out_hbm, buffer, sems, f, form=NT):
    pair = both.shape[1]
    rows = both.shape[0] // 2
    value = lax.dot_general(both, right, form, preferred_element_type=F32) * (2.0 / pair)
    value = value.astype(BF16)
    buffer[f, 0] = value[:rows]
    buffer[f, 1] = value[rows:]
    copy = pltpu.make_async_copy(buffer.at[f], out_hbm.at[0, f], sems.at[f])
    copy.start()
    return copy


def auto_kernel(otm_ref, picked_ref, csd_hbm, left_ref, buffer, sems):
    lines = buffer.shape[0]
    cross = left_ref.shape[0] // 2
    z = lax.dot_general(otm_ref[...], picked_ref[...], TN, preferred_element_type=F32)
    z = z.astype(BF16)
    pair = z.shape[1] // lines
    copies = []
    for f in range(lines):
        line = z[:, f * pair : (f + 1) * pair]
        left_ref[: cross, f * pair : (f + 1) * pair] = line[:cross]
        left_ref[cross :, f * pair : (f + 1) * pair] = turned(line[:cross])
        copies.append(spectra(jnp.concatenate([line, turned(line)], axis=0), line, csd_hbm, buffer, sems, f))
    for copy in copies:
        copy.wait()


def joint_kernel(left_ref, joined_ref, joint_hbm, buffer, sems):
    lines = buffer.shape[0]
    columns = left_ref.shape[1]
    z = lax.dot_general(
        joined_ref[:, :columns], joined_ref[:, columns:], TN, preferred_element_type=F32
    )
    z = z.astype(BF16)
    pair = columns // lines
    copies = []
    for f in range(lines):
        part = slice(f * pair, (f + 1) * pair)
        copies.append(
            spectra(left_ref[:, part], z[part], joint_hbm, buffer, sems, f, NN)
        )
    for copy in copies:
        copy.wait()


def per_device(mode_shapes, modal_freq, damping, excitation, modal_load, attach, row_count, otm):
    count = lax.axis_size("mode")
    half = count // 2
    iface, modes = mode_shapes.shape
    rows_max, att = otm.shape[1], otm.shape[2]
    lines = excitation.shape[0]
    pair = 2 * modal_load.shape[3]
    columns = lines * pair
    vmem = pl.BlockSpec(memory_space=pltpu.VMEM)
    hbm = pl.BlockSpec(memory_space=pl.ANY)
    load_t = jnp.transpose(modal_load, (1, 2, 3, 0))
    otm_t = jnp.transpose(otm[0], (1, 0))
    part = pltpu.VMEM((att, columns), BF16)
    part_wide = pltpu.VMEM((att, columns), F32)
    chunks = CHUNKS if iface % (16 * CHUNKS) == 0 else 1
    pieces = modes // LANES
    steps = list(range(half - 1, 0, -1))
    slots = [half ^ k for k in steps] + [half] + steps + [0]
    outs = pl.pallas_call(
        functools.partial(parts_kernel, slots),
        out_shape=([part] * (half - 1) + [part_wide]) * 2,
        in_specs=[hbm] * 6,
        out_specs=[vmem] * count,
        scratch_shapes=[
            pltpu.SMEM(attach.shape, jnp.int32),
            pltpu.SMEM(excitation.shape, F32),
            pltpu.VMEM(modal_freq.shape, F32),
            pltpu.VMEM(damping.shape, F32),
            pltpu.VMEM(load_t.shape, F32),
            pltpu.VMEM((iface, modes), BF16),
            pltpu.VMEM((iface * pieces + SPARE, LANES), F32),
            pltpu.VMEM((count * att * pieces + SPARE, LANES), F32),
            pltpu.VMEM((columns, modes), BF16),
            pltpu.SemaphoreType.DMA((chunks,)),
            pltpu.SemaphoreType.DMA((5,)),
        ],
        compiler_params=pltpu.CompilerParams(vmem_limit_bytes=58 << 20),
        name="partial_sums",
    )(attach, excitation, modal_freq, damping, load_t, mode_shapes)
    far, far_own = list(outs[: half - 1]), outs[half - 1]
    near, near_own = list(outs[half : count - 1]), outs[count - 1]
    used = jnp.arange(rows_max, dtype=jnp.int32)[None, :] < row_count[:, None]
    own_otm = jnp.where(used, otm_t, jnp.zeros_like(otm_t))

    def swapped(value, k):
        return lax.ppermute(value, "mode", [(i, i ^ k) for i in range(count)])

    def following(value):
        return lax.ppermute(value, "mode", [(i, i - 1) for i in range(1, count)])

    far_sum = far_own
    for k, value in zip(steps, far):
        far_sum = far_sum + swapped(value, k).astype(F32)
    picked = near_own
    for k, value in zip(steps, near):
        picked = picked + swapped(value, k).astype(F32)
    far_sum, own_otm = lax.optimization_barrier((far_sum.astype(BF16), own_otm))
    picked = picked + swapped(far_sum, half).astype(F32)
    picked = picked.astype(BF16)
    joined = following(jnp.concatenate([picked, own_otm], axis=1))

    params = pltpu.CompilerParams(vmem_limit_bytes=24 << 20)
    csd, left = pl.pallas_call(
        auto_kernel,
        out_shape=[
            jax.ShapeDtypeStruct((1, lines, 2, rows_max, rows_max), BF16),
            jax.ShapeDtypeStruct((2 * CROSS, columns), BF16),
        ],
        in_specs=[vmem] * 2,
        out_specs=[hbm, vmem],
        scratch_shapes=[
            pltpu.VMEM((lines, 2, rows_max, rows_max), BF16),
            pltpu.SemaphoreType.DMA((lines,)),
        ],
        compiler_params=params,
        name="auto_csd",
    )(own_otm, picked)
    joint = pl.pallas_call(
        joint_kernel,
        out_shape=jax.ShapeDtypeStruct((1, lines, 2, CROSS, rows_max), BF16),
        in_specs=[vmem] * 2,
        out_specs=hbm,
        scratch_shapes=[
            pltpu.VMEM((lines, 2, CROSS, rows_max), BF16),
            pltpu.SemaphoreType.DMA((lines,)),
        ],
        compiler_params=params,
        name="joint_csd",
    )(left, joined)
    return (csd, joint)


def solution(mesh):
    return jax.shard_map(
        per_device,
        mesh=mesh,
        in_specs=(
            P(None, "mode"),
            P("mode"),
            P("mode"),
            P("freq"),
            P("mode", "freq", None, None),
            P(),
            P("mode"),
            P("mode", None, None),
        ),
        out_specs=(P("mode", "freq", None, None, None), P("mode", "freq", None, None, None)),
        check_vma=False,
    )
```
